256 devices in a mesh: rows: 128 (over x, y, z_hi, core), rep: 2 (over z_lo).
Axes of the slice: x: 4, y: 4, z: 8 (z_hi: 4, z_lo: 2; z = z_hi * 2 + z_lo), core: 2. Of those that a mesh axis runs over, the one named last changes fastest.
Arguments:
- features: bfloat16 [32768, 128], P('rows'), may hold values from -6 to 6
- node_order: int32 [32768], P('rows'), may hold values from 0 to 32767, as said below
- tile_vals: bfloat16 [49152, 128, 128], P(('rows', 'rep')), may hold values from -0.0546875 to 0.0546875
- tile_row: int32 [49152], P(('rows', 'rep')), may hold values from 0 to 255, as said below
- tile_col: int32 [49152], P(('rows', 'rep')), may hold values from 0 to 255, as said below
- tile_count: int32 [256], P(('rows', 'rep')), may hold values from 48 to 192, as said below
- weight: bfloat16 [128, 256], replicated, may hold values from -0.5 to 0.5
- bias: float32 [256], replicated, may hold values from -3 to 3
- cotangent: bfloat16 [32768, 256], P('rows'), may hold values from -6 to 6
Outputs:
- activations: bfloat16 [32768, 256], P('rows')
- weight_grad: float32 [128, 256], replicated
- bias_grad: float32 [256], replicated
The draws below stay inside these ranges and needn't reach their ends.
Inputs may be any that keep to these rules, and one draw needn't show every extreme that they name: `node_order`: positions c * 256 to c * 256 + 255 hold each of the node numbers c * 256 to c * 256 + 255 once. `tile_row`: slots d * 192 to d * 192 + 191 belong to device d = i * 2 + j (i along rows, j along rep); each of them names a row-block from i * 2 to i * 2 + 1. `tile_col`: A slot of device d = i * 2 + j names a column-block c * 2 + j + e for any node group c and any e from 0 to 0; slots may repeat a pair of row-block and column-block. Only the first tile_count[d] slots of device d are live; some device has exactly 192 and some other exactly 48.
All inputs are finite; a program needn't handle non-finite values.
Results may differ from the reference program's by a relative error of at most 0.0056.
Values may be sent and summed in bfloat16 or wider, within the bound.
No kernel may reach another device: no remote copies, remote signals or barrier semaphores. Data moves between devices by JAX's collectives and lax.ppermute only.
A program may use at most 128 MiB of HBM per device.

```python
import jax
import jax.numpy as jnp
from jax import lax

F_IN = 128
HID = 256
BLOCK = 128
RB_DEV = 2
TILES_DEV = 192
REPLICAS = 2
NODES_DEV = 256
NB = 256
NODES = 32768
N_ROWS = 128
N_REP = 2
DEVICES = 256


def draw_node_order(key, part):
    group_count = NODES // NODES_DEV
    seg_keys = jax.random.split(jax.random.fold_in(key, 5), group_count)
    segments = jax.vmap(lambda single: jax.random.permutation(single, NODES_DEV))(seg_keys)
    offsets = (jnp.arange(group_count, dtype=jnp.int32) * NODES_DEV)[:, None]
    return (segments.astype(jnp.int32) + offsets).reshape(NODES)


def draw_tile_row(key, part):
    slot_total = DEVICES * TILES_DEV
    device = jnp.arange(slot_total, dtype=jnp.int32) // TILES_DEV
    row_group = device // REPLICAS
    choose = jax.random.randint(jax.random.fold_in(key, 3), (slot_total,), 0, RB_DEV, dtype=jnp.int32)
    return row_group * RB_DEV + choose


def draw_tile_col(key, part):
    slot_total = DEVICES * TILES_DEV
    device = jnp.arange(slot_total, dtype=jnp.int32) // TILES_DEV
    replica = device % REPLICAS
    half_blocks = RB_DEV // REPLICAS
    owner_key, within_key = jax.random.split(jax.random.fold_in(key, 7))
    owner = jax.random.randint(owner_key, (slot_total,), 0, DEVICES // REPLICAS, dtype=jnp.int32)
    within = jax.random.randint(within_key, (slot_total,), 0, half_blocks, dtype=jnp.int32)
    return owner * RB_DEV + replica * half_blocks + within


def draw_tile_count(key, part):
    first_key, second_key, third_key = jax.random.split(jax.random.fold_in(key, 11), 3)
    counts = jax.random.randint(first_key, (DEVICES,), TILES_DEV // 4, TILES_DEV + 1, dtype=jnp.int32)
    busiest = jax.random.randint(second_key, (), 0, DEVICES, dtype=jnp.int32)
    lightest = (busiest + jax.random.randint(third_key, (), 1, DEVICES, dtype=jnp.int32)) % DEVICES
    counts = counts.at[busiest].set(TILES_DEV)
    counts = counts.at[lightest].set(TILES_DEV // 4)
    return counts


def shard_levels(own_key, shape, cuts, low, largest):
    level = 1.0
    for position, shards_of in cuts:
        heights = jax.random.uniform(jax.random.fold_in(jax.random.fold_in(own_key, 6), position), (shards_of,), jnp.float32, low / len(cuts), largest / len(cuts))
        level = level * jnp.repeat(jnp.exp(heights), shape[position] // shards_of).reshape((-1,) + (1,) * (len(shape) - 1 - position))
    return level


def centred(rng, dims, spread, limit, cuts=(), kind=jnp.bfloat16):
    drawn = jax.random.normal(rng, dims, jnp.float32) * spread
    if len(cuts) > 0:
        drawn = shard_levels(rng, dims, cuts, -0.22, 0.18) * drawn
    return jnp.clip(drawn, min=-limit, max=limit).astype(kind)


def setup_inputs(seed: int = 0) -> dict:
    keys = jax.random.split(jax.random.key(seed), 10)
    return {
        "features": centred(keys[0], (NODES, F_IN), 1.0, 6.0, ((0, 128),)),
        "node_order": draw_node_order(jax.random.fold_in(keys[9], 71), 0),
        "tile_vals": centred(keys[2], (DEVICES * TILES_DEV, BLOCK, BLOCK), (BLOCK * TILES_DEV // RB_DEV) ** -0.5, 0.0546875, ((0, 256),)),
        "tile_row": draw_tile_row(jax.random.fold_in(keys[9], 71), 0),
        "tile_col": draw_tile_col(jax.random.fold_in(keys[9], 71), 0),
        "tile_count": draw_tile_count(jax.random.fold_in(keys[9], 71), 0),
        "weight": centred(keys[6], (F_IN, HID), F_IN ** -0.5, 0.5),
        "bias": centred(keys[7], (HID,), 0.5, 3.0, (), jnp.float32),
        "cotangent": centred(keys[8], (NODES, HID), 1.0, 6.0, ((0, 128),)),
    }


def silu_slope(pre_act):
    sigma = jax.nn.sigmoid(pre_act)
    return sigma * (1.0 + pre_act * (1.0 - sigma))


def reference(features, node_order, tile_vals, tile_row, tile_col, tile_count, weight, bias, cotangent):
    reordered = features[node_order]
    blocks = reordered.reshape(NB, BLOCK, F_IN)
    tile_stack = tile_vals.reshape(DEVICES, TILES_DEV, BLOCK, BLOCK)
    row_table = tile_row.reshape(DEVICES, TILES_DEV)
    col_table = tile_col.reshape(DEVICES, TILES_DEV)

    def one_device(packed):
        device, tile_set, row_ids, col_ids, tile_total = packed
        live_mask = (jnp.arange(TILES_DEV, dtype=jnp.int32) < tile_total).astype(jnp.float32)
        sources = blocks[col_ids].astype(jnp.float32)
        products = jnp.einsum("tij,tjf->tif", tile_set.astype(jnp.float32), sources, precision=lax.Precision.HIGHEST)
        owner_row = device // N_REP
        local_rows = row_ids - owner_row * RB_DEV
        select = (local_rows[:, None] == jnp.arange(RB_DEV, dtype=jnp.int32)[None, :]).astype(jnp.float32)
        select = select * live_mask[:, None]
        return jnp.einsum("tk,tif->kif", select, products, precision=lax.Precision.HIGHEST)

    partial_value = lax.map(one_device, (jnp.arange(DEVICES, dtype=jnp.int32), tile_stack, row_table, col_table, tile_count))
    summed = partial_value.reshape(N_ROWS, N_REP, NODES_DEV, F_IN).sum(axis=1)
    hidden = summed.reshape(NODES, F_IN).astype(jnp.bfloat16)
    pre_act = jnp.dot(hidden, weight, preferred_element_type=jnp.float32) + bias.astype(jnp.float32)
    activated = jax.nn.silu(pre_act).astype(jnp.bfloat16)
    activations = jnp.zeros((NODES, HID), jnp.bfloat16).at[node_order].set(activated)
    grad_reordered = cotangent[node_order].astype(jnp.float32)
    scaled = (grad_reordered * silu_slope(pre_act)).astype(jnp.bfloat16)
    grad_scale = float(NODES) ** -0.5
    weight_grad = lax.dot_general(hidden, scaled, (((0,), (0,)), ((), ())), preferred_element_type=jnp.float32) * grad_scale
    bias_grad = jnp.sum(scaled.astype(jnp.float32), axis=0) * grad_scale
    return activations, weight_grad, bias_grad
```

```python
import itertools

import jax
import jax.numpy as jnp
from jax import lax
from jax.experimental import pallas as pl
from jax.experimental.pallas import tpu as pltpu
from jax.sharding import Mesh
from jax.sharding import PartitionSpec as P

ROWS = ("x", "y", "z", "c")
ROWS_REP = ("x", "y", "z", "c", "rep")
GROUP = 4

SMEM = pl.BlockSpec(memory_space=pltpu.SMEM)
VMEM = pl.BlockSpec(memory_space=pltpu.VMEM)


def swap(value, axis, step):
    n = lax.axis_size(axis)
    return lax.ppermute(value, axis, [(i, i ^ step) for i in range(n)])


def swap_plane(value, step, last):
    nx, ny = lax.axis_size("x"), lax.axis_size("y")
    pairs = []
    for x, y, c in itertools.product(range(nx), range(ny), range(2)):
        along_x = (c == 1) != last
        x2, y2 = (x ^ step, y) if along_x else (x, y ^ step)
        pairs.append(((x * ny + y) * 2 + c, (x2 * ny + y2) * 2 + c))
    return lax.ppermute(value, ("x", "y", "c"), pairs)


def reorder_kernel(place, order, features, own):
    half = own.shape[0]
    nodes = features.shape[0]
    wanted = order[pl.ds(place[1], 1), :] & (nodes - 1)
    pick = (lax.broadcasted_iota(jnp.int32, (nodes, half), 0) == wanted).astype(jnp.bfloat16)
    own[...] = lax.dot_general(
        pick, features[...], (((0,), (0,)), ((), ())), preferred_element_type=jnp.float32
    ).astype(jnp.bfloat16)


def tiles_kernel(position, row, count, tiles, *refs):
    pieces, (out, sources) = refs[:-2], refs[-2:]
    size = tiles.shape[1]
    live = count[0]
    blocks = pieces[0].shape[0]

    def place_block(b, _):
        for k, piece in enumerate(pieces):
            sources[k * blocks + b] = piece[b]
        return 0

    lax.fori_loop(0, blocks, place_block, 0)

    def step(g, total):
        lefts, rights = [], []
        for k in range(GROUP):
            t = g * GROUP + k
            block = sources[position[t]]
            zero = jnp.zeros_like(block)
            first = jnp.where((row[t] == 0) & (t < live), block, zero)
            second = jnp.where((row[t] == 1) & (t < live), block, zero)
            lefts.append(tiles[t])
            rights.append(jnp.concatenate([first, second], axis=1))
        return total + jnp.dot(
            jnp.concatenate(lefts, axis=1),
            jnp.concatenate(rights, axis=0),
            preferred_element_type=jnp.float32,
        )

    total = lax.fori_loop(
        0, (live + GROUP - 1) // GROUP, step, jnp.zeros((size, 2 * size), jnp.float32)
    )
    out[:size] = total[:, :size]
    out[size:] = total[:, size:]


def dense_kernel(place, order, mine, theirs, weight, bias, cotangent, act, keep, send):
    nodes = mine.shape[0]
    half = weight.shape[1] // 2
    part = weight.shape[0] // 2
    hidden = (mine[...] + theirs[...]).astype(jnp.bfloat16)
    where = jnp.concatenate([order[0:1], order[1:2]], axis=1) & (nodes - 1)
    put = (lax.broadcasted_iota(jnp.int32, (nodes, nodes), 0) == where).astype(jnp.bfloat16)
    hidden = jnp.dot(put, hidden, preferred_element_type=jnp.float32).astype(jnp.bfloat16)
    pre_act = jnp.dot(hidden, weight[...], preferred_element_type=jnp.float32) + bias[...]
    sigma = 1.0 / (1.0 + jnp.exp(-pre_act))
    act[...] = (pre_act * sigma).astype(jnp.bfloat16)
    slope = sigma * (1.0 + pre_act * (1.0 - sigma))
    scaled = (cotangent[...].astype(jnp.float32) * slope).astype(jnp.bfloat16)
    total = lax.dot_general(
        hidden, scaled, (((0,), (0,)), ((), ())), preferred_element_type=jnp.float32
    )
    column = jnp.sum(scaled.astype(jnp.float32), axis=0, keepdims=True)
    upper = place[1] == 1
    total = jnp.where(upper, total[:, half:], total[:, :half])
    column = jnp.where(upper, column[:, half:], column[:, :half])
    lower = place[0] == 0
    keep[:part] = jnp.where(lower, total[:part], total[part:])
    send[:part] = jnp.where(lower, total[part:], total[:part])
    keep[part:] = jnp.broadcast_to(column, (8, half))
    send[part:] = jnp.broadcast_to(column, (8, half))


def finish_kernel(scale, place, own, core, rep, both, weight_grad, bias_grad):
    part = own.shape[0] - 8
    half = own.shape[1]
    c, j = place[0], place[1]
    for piece, c2, j2 in ((own, c, j), (core, 1 - c, j), (rep, c, 1 - j), (both, 1 - c, 1 - j)):
        rows = pl.ds(pl.multiple_of(c2 * part, part), part)
        columns = pl.ds(pl.multiple_of(j2 * half, half), half)
        weight_grad[rows, columns] = piece[:part] * scale
    for piece, j2 in ((own, j), (rep, 1 - j)):
        columns = pl.ds(pl.multiple_of(j2 * half, half), half)
        bias_grad[:, columns] = piece[part : part + 1] * scale


def gathered(own):
    v = own[None]
    v = jnp.concatenate([v, swap(v, "z", 1)])
    v = jnp.concatenate([v, swap(v, "z", 3)])
    v = jnp.concatenate([v] + [swap_plane(v, s, False) for s in (1, 2, 3)])
    pieces = [v] + [swap_plane(v, s, True) for s in (1, 2, 3)]
    return pieces + [swap(p, "c", 1) for p in pieces]


def positions(tile_col, me):
    source = tile_col >> 1
    away = source ^ me
    x, y, z, c = (away >> 5) & 3, (away >> 3) & 3, (away >> 1) & 3, away & 1
    flip = (source & 1) == 1
    last, plane = jnp.where(flip, y, x), jnp.where(flip, x, y)
    return c * 64 + last * 16 + plane * 4 + (z ^ (z >> 1))


def body(features, node_order, tile_vals, tile_row, tile_col, tile_count, weight, bias, cotangent):
    nodes, width = features.shape
    slots, size, _ = tile_vals.shape
    hid = weight.shape[1]
    half, part = hid // 2, width // 2
    me = lax.axis_index(ROWS)
    place = jnp.stack([lax.axis_index("c"), lax.axis_index("rep")]).astype(jnp.int32)
    order = node_order.reshape(2, nodes // 2)
    own = pl.pallas_call(
        reorder_kernel,
        out_shape=jax.ShapeDtypeStruct((nodes // 2, width), jnp.bfloat16),
        in_specs=[SMEM, VMEM, VMEM],
        out_specs=VMEM,
        compiler_params=pltpu.CompilerParams(vmem_limit_bytes=4 * 2**20),
    )(place, order, features)
    pieces = gathered(own)
    blocks = len(pieces) * pieces[0].shape[0]
    mine = pl.pallas_call(
        tiles_kernel,
        out_shape=jax.ShapeDtypeStruct((nodes, width), jnp.float32),
        in_specs=[SMEM] * 3 + [VMEM] * (1 + len(pieces)),
        out_specs=VMEM,
        scratch_shapes=[pltpu.VMEM((blocks, size, width), jnp.bfloat16)],
        compiler_params=pltpu.CompilerParams(vmem_limit_bytes=32 * 2**20),
    )(positions(tile_col, me), tile_row & 1, tile_count, tile_vals, *pieces)
    theirs = swap(mine, "rep", 1)
    act, keep, send = pl.pallas_call(
        dense_kernel,
        out_shape=(
            jax.ShapeDtypeStruct((nodes, hid), jnp.bfloat16),
            jax.ShapeDtypeStruct((part + 8, half), jnp.float32),
            jax.ShapeDtypeStruct((part + 8, half), jnp.float32),
        ),
        in_specs=[SMEM] + [VMEM] * 6,
        out_specs=(VMEM,) * 3,
        compiler_params=pltpu.CompilerParams(vmem_limit_bytes=16 * 2**20),
    )(place, order, mine, theirs, weight, bias.reshape(1, hid), cotangent)
    total = keep + swap(send, "c", 1)
    for axis in ("z", "y", "x"):
        for step in (1, 3):
            total = total + swap(total, axis, step)
    scale = float(nodes * lax.axis_size(ROWS)) ** -0.5
    weight_grad, bias_grad = pl.pallas_call(
        lambda *refs: finish_kernel(scale, *refs),
        out_shape=(
            jax.ShapeDtypeStruct((width, hid), jnp.float32),
            jax.ShapeDtypeStruct((1, hid), jnp.float32),
        ),
        in_specs=[SMEM] + [VMEM] * 4,
        out_specs=(VMEM,) * 2,
        compiler_params=pltpu.CompilerParams(vmem_limit_bytes=4 * 2**20),
    )(
        place,
        total,
        swap(total, "c", 1),
        swap(total, "rep", 1),
        swap(total, ("c", "rep"), 3),
    )
    return act, weight_grad, bias_grad.reshape(hid)


def solution(mesh):
    finer = Mesh(mesh.devices.reshape(4, 4, 4, 2, mesh.shape["rep"]), ROWS_REP)
    return jax.shard_map(
        body,
        mesh=finer,
        in_specs=(
            P(ROWS, None),
            P(ROWS),
            P(ROWS_REP, None, None),
            P(ROWS_REP),
            P(ROWS_REP),
            P(ROWS_REP),
            P(),
            P(),
            P(ROWS, None),
        ),
        out_specs=(P(ROWS, None), P(), P()),
        check_vma=False,
    )
```

```python
import functools
import itertools

import jax
import jax.numpy as jnp
from jax import lax
from jax.experimental import pallas as pl
from jax.experimental.pallas import tpu as pltpu
from jax.sharding import Mesh
from jax.sharding import PartitionSpec as P

ROWS = ("x", "y", "z", "c")
ROWS_REP = ("x", "y", "z", "c", "rep")
GROUP = 8
KINDS = 6
EMPTY = 48

SMEM = pl.BlockSpec(memory_space=pltpu.SMEM)
VMEM = pl.BlockSpec(memory_space=pltpu.VMEM)


def swap(value, axis, step):
    n = lax.axis_size(axis)
    return lax.ppermute(value, axis, [(i, i ^ step) for i in range(n)])


def swap_plane(value, step, last):
    nx, ny = lax.axis_size("x"), lax.axis_size("y")
    pairs = []
    for x, y, c in itertools.product(range(nx), range(ny), range(2)):
        along_x = (c == 1) != last
        x2, y2 = (x ^ step, y) if along_x else (x, y ^ step)
        pairs.append(((x * ny + y) * 2 + c, (x2 * ny + y2) * 2 + c))
    return lax.ppermute(value, ("x", "y", "c"), pairs)


def reorder_kernel(rep, order, features, own):
    half = own.shape[0]
    nodes = features.shape[0]
    wanted = order[pl.ds(rep[0], 1), :] & (nodes - 1)
    pick = (lax.broadcasted_iota(jnp.int32, (nodes, half), 0) == wanted).astype(jnp.bfloat16)
    own[...] = lax.dot_general(
        pick, features[...], (((0,), (0,)), ((), ())), preferred_element_type=jnp.float32
    ).astype(jnp.bfloat16)


def plan_kernel(kind, place, count, order, spot, groups, filled):
    room = order.shape[0] // KINDS
    for n in range(KINDS):
        filled[n] = n * room

    def step(t, carry):
        n = kind[t]
        at = filled[n]
        order[at] = t
        spot[at] = place[t]
        filled[n] = at + 1
        return carry

    lax.fori_loop(0, count[0], step, 0)

    def finish(n, carry):
        end = filled[n]
        for k in range(GROUP):
            order[end + k] = 0
            spot[end + k] = EMPTY
        groups[n] = (end - n * room + GROUP - 1) // GROUP
        return carry

    lax.fori_loop(0, KINDS, finish, 0)


def tiles_kernel(kind, order, spot, groups, tiles, *refs):
    refs, out, sources = refs[:-2], refs[-2], refs[-1]
    size = tiles.shape[1]
    before = None
    if refs[0].shape == out.shape:
        before, refs = refs[0], refs[1:]
    blocks = refs[0].shape[0]
    room = order.shape[0] // KINDS

    def place_block(b, carry):
        for k, piece in enumerate(refs):
            sources[k * blocks + b] = piece[b]
        return carry

    lax.fori_loop(0, blocks, place_block, 0)
    sources[EMPTY] = jnp.zeros((size, size), jnp.bfloat16)

    for r in range(2):
        rows = slice(r * size, (r + 1) * size)

        def step(q, acc):
            at = (kind + r) * room + q * GROUP
            left = jnp.concatenate([tiles[order[at + k]] for k in range(GROUP)], axis=1)
            right = jnp.concatenate([sources[spot[at + k]] for k in range(GROUP)], axis=0)
            return acc + jnp.dot(left, right, preferred_element_type=jnp.float32)

        start = jnp.zeros((size, size), jnp.float32) if before is None else before[rows]
        out[rows] = lax.fori_loop(0, groups[kind + r], step, start)


def dense_kernel(core, rep, order, mine, theirs, weight, bias, cotangent, act, keep, send):
    nodes = mine.shape[0]
    half = weight.shape[1] // 2
    part = weight.shape[0] // 2
    hidden = (mine[...] + theirs[...]).astype(jnp.bfloat16)
    where = jnp.concatenate([order[0:1], order[1:2]], axis=1) & (nodes - 1)
    put = (lax.broadcasted_iota(jnp.int32, (nodes, nodes), 0) == where).astype(jnp.bfloat16)
    hidden = jnp.dot(put, hidden, preferred_element_type=jnp.float32).astype(jnp.bfloat16)
    pre_act = jnp.dot(hidden, weight[...], preferred_element_type=jnp.float32) + bias[...]
    sigma = 1.0 / (1.0 + jnp.exp(-pre_act))
    act[...] = (pre_act * sigma).astype(jnp.bfloat16)
    slope = sigma * (1.0 + pre_act * (1.0 - sigma))
    scaled = (cotangent[...].astype(jnp.float32) * slope).astype(jnp.bfloat16)
    total = lax.dot_general(
        hidden, scaled, (((0,), (0,)), ((), ())), preferred_element_type=jnp.float32
    )
    column = jnp.sum(scaled.astype(jnp.float32), axis=0, keepdims=True)
    upper = rep[0] == 1
    total = jnp.where(upper, total[:, half:], total[:, :half])
    column = jnp.where(upper, column[:, half:], column[:, :half])
    lower = core[0] == 0
    keep[:part] = jnp.where(lower, total[:part], total[part:])
    send[:part] = jnp.where(lower, total[part:], total[:part])
    keep[part:] = jnp.broadcast_to(column, (8, half))
    send[part:] = jnp.broadcast_to(column, (8, half))


def pair_kernel(core, own, other, out):
    part = own.shape[0] - 8
    lower = core[0] == 0
    out[:part] = jnp.where(lower, own[:part], other[:part])
    out[part : 2 * part] = jnp.where(lower, other[:part], own[:part])
    out[2 * part :] = own[part:]


def finish_kernel(scale, rep, own, other, weight_grad, bias_grad):
    width, half = own.shape[0] - 8, own.shape[1]
    left = rep[0] == 0
    for columns, first, second in ((slice(0, half), own, other), (slice(half, 2 * half), other, own)):
        weight_grad[:, columns] = jnp.where(left, first[:width], second[:width]) * scale
        bias_grad[:, columns] = jnp.where(left, first[width : width + 1], second[width : width + 1]) * scale


def kinds_and_places(tile_row, tile_col, me):
    source = tile_col >> 1
    away = source ^ me
    x, y, z, c = (away >> 5) & 3, (away >> 3) & 3, (away >> 1) & 3, away & 1
    flip = (source & 1) == 1
    last, plane = jnp.where(flip, y, x), jnp.where(flip, x, y)
    early = last == 0
    kind = jnp.where(early, 0, 2 + 2 * c) + (tile_row & 1)
    return kind, jnp.where(early, c, last - 1) * 16 + plane * 4 + z


def aggregated(own, me, tile_vals, tile_row, tile_col, tile_count):
    slots, size, _ = tile_vals.shape
    width = own.shape[1]

    def products(kind, before, pieces):
        before = [] if before is None else [before]
        return pl.pallas_call(
            functools.partial(tiles_kernel, kind),
            out_shape=jax.ShapeDtypeStruct((2 * size, width), jnp.float32),
            in_specs=[SMEM] * 3 + [VMEM] * (1 + len(before) + len(pieces)),
            out_specs=VMEM,
            scratch_shapes=[pltpu.VMEM((EMPTY + 1, size, width), jnp.bfloat16)],
            compiler_params=pltpu.CompilerParams(vmem_limit_bytes=8 * 2**20),
            cost_estimate=pl.CostEstimate(
                flops=128 * size**3, bytes_accessed=64 * 2 * size**2, transcendentals=0
            ),
        )(*plan, tile_vals, *before, *pieces)

    line = jnp.concatenate([own[None]] + [swap(own[None], "z", s) for s in (1, 2, 3)])
    line = lax.optimization_barrier(line)
    plane = jnp.concatenate([line] + [swap_plane(line, s, False) for s in (1, 2, 3)])
    plane = lax.optimization_barrier(plane)
    one, two, three = (swap_plane(plane, s, True) for s in (1, 2, 3))
    other = swap(plane, "c", 1)

    row, col, _ = lax.optimization_barrier((tile_row, tile_col, plane))
    kind, place = kinds_and_places(row, col, me)
    entries = jax.ShapeDtypeStruct((KINDS * (slots + GROUP),), jnp.int32)
    plan = pl.pallas_call(
        plan_kernel,
        out_shape=(entries, entries, jax.ShapeDtypeStruct((KINDS,), jnp.int32)),
        in_specs=[SMEM] * 3,
        out_specs=(SMEM,) * 3,
        scratch_shapes=[pltpu.SMEM((KINDS,), jnp.int32)],
        compiler_params=pltpu.CompilerParams(vmem_limit_bytes=4 * 2**20),
    )(kind, place, tile_count)
    total = products(0, None, [plane, other])
    one, two, three, total = lax.optimization_barrier((one, two, three, total))
    others = [swap(p, "c", 1) for p in (one, two, three)]
    total = products(2, total, [one, two, three])
    return products(4, total, others)


def body(features, node_order, tile_vals, tile_row, tile_col, tile_count, weight, bias, cotangent):
    nodes, width = features.shape
    hid = weight.shape[1]
    half, part = hid // 2, width // 2
    me = lax.axis_index(ROWS)
    core = lax.axis_index("c").reshape(1)
    rep = lax.axis_index("rep").reshape(1)
    order = node_order.reshape(2, nodes // 2)
    own = pl.pallas_call(
        reorder_kernel,
        out_shape=jax.ShapeDtypeStruct((nodes // 2, width), jnp.bfloat16),
        in_specs=[SMEM, VMEM, VMEM],
        out_specs=VMEM,
        compiler_params=pltpu.CompilerParams(vmem_limit_bytes=56 * 2**20),
    )(rep, order, features)

    mine = aggregated(own, me, tile_vals, tile_row, tile_col, tile_count)
    theirs = swap(mine, "rep", 1)
    act, keep, send = pl.pallas_call(
        dense_kernel,
        out_shape=(
            jax.ShapeDtypeStruct((nodes, hid), jnp.bfloat16),
            jax.ShapeDtypeStruct((part + 8, half), jnp.float32),
            jax.ShapeDtypeStruct((part + 8, half), jnp.float32),
        ),
        in_specs=[SMEM] * 2 + [VMEM] * 6,
        out_specs=(VMEM,) * 3,
        compiler_params=pltpu.CompilerParams(vmem_limit_bytes=16 * 2**20),
    )(core, rep, order, mine, theirs, weight, bias.reshape(1, hid), cotangent)
    total = keep + swap(send, "c", 1)
    for axis in ("z", "y", "x"):
        one, two, three = (swap(total, axis, step) for step in (1, 2, 3))
        total = (total + one) + (two + three)
    scale = float(nodes * lax.axis_size(ROWS)) ** -0.5
    pair = pl.pallas_call(
        pair_kernel,
        out_shape=jax.ShapeDtypeStruct((width + 8, half), jnp.float32),
        in_specs=[SMEM] + [VMEM] * 2,
        out_specs=VMEM,
        compiler_params=pltpu.CompilerParams(vmem_limit_bytes=4 * 2**20),
    )(core, total, swap(total, "c", 1))
    weight_grad, bias_grad = pl.pallas_call(
        functools.partial(finish_kernel, scale),
        out_shape=(
            jax.ShapeDtypeStruct((width, hid), jnp.float32),
            jax.ShapeDtypeStruct((1, hid), jnp.float32),
        ),
        in_specs=[SMEM] + [VMEM] * 2,
        out_specs=(VMEM,) * 2,
        compiler_params=pltpu.CompilerParams(vmem_limit_bytes=4 * 2**20),
    )(rep, pair, swap(pair, "rep", 1))
    return act, weight_grad, bias_grad.reshape(hid)


def solution(mesh):
    finer = Mesh(mesh.devices.reshape(4, 4, 4, 2, mesh.shape["rep"]), ROWS_REP)
    return jax.shard_map(
        body,
        mesh=finer,
        in_specs=(
            P(ROWS, None),
            P(ROWS),
            P(ROWS_REP, None, None),
            P(ROWS_REP),
            P(ROWS_REP),
            P(ROWS_REP),
            P(),
            P(),
            P(ROWS, None),
        ),
        out_specs=(P(ROWS, None), P(), P()),
        check_vma=False,
    )
```

```python
import functools
import itertools

import jax
import jax.numpy as jnp
from jax import lax
from jax.experimental import pallas as pl
from jax.experimental.pallas import tpu as pltpu
from jax.sharding import Mesh
from jax.sharding import PartitionSpec as P

ROWS = ("x", "y", "z", "c")
ROWS_REP = ("x", "y", "z", "c", "rep")
GROUP = 8
KINDS = 6
EMPTY = 48

SMEM = pl.BlockSpec(memory_space=pltpu.SMEM)
VMEM = pl.BlockSpec(memory_space=pltpu.VMEM)


def swap(value, axis, step):
    n = lax.axis_size(axis)
    return lax.ppermute(value, axis, [(i, i ^ step) for i in range(n)])


def swap_by_core(value, axes, step):
    names = ("x", "y", "z", "c")
    shape = [lax.axis_size(name) for name in names]
    pairs = []
    for source, index in enumerate(itertools.product(*map(range, shape))):
        at = names.index(axes[index[3]])
        target = 0
        for place, (size, i) in enumerate(zip(shape, index)):
            target = target * size + (i ^ step if place == at else i)
        pairs.append((source, target))
    return lax.ppermute(value, names, pairs)


def reorder_kernel(rep, order, features, own):
    half = own.shape[0]
    nodes = features.shape[0]
    wanted = order[pl.ds(rep[0], 1), :] & (nodes - 1)
    pick = (lax.broadcasted_iota(jnp.int32, (nodes, half), 0) == wanted).astype(jnp.bfloat16)
    own[...] = lax.dot_general(
        pick, features[...], (((0,), (0,)), ((), ())), preferred_element_type=jnp.float32
    ).astype(jnp.bfloat16)


def plan_kernel(kind, place, count, order, spot, groups, filled):
    room = order.shape[0] // KINDS
    for n in range(KINDS):
        filled[n] = n * room

    def step(t, carry):
        n = kind[t]
        at = filled[n]
        order[at] = t
        spot[at] = place[t]
        filled[n] = at + 1
        return carry

    lax.fori_loop(0, count[0], step, 0)

    def finish(n, carry):
        end = filled[n]
        for k in range(2 * GROUP):
            order[end + k] = 0
            spot[end + k] = EMPTY
        groups[n] = (end - n * room + GROUP - 1) // GROUP
        return carry

    lax.fori_loop(0, KINDS, finish, 0)


def tiles_kernel(kind, order, spot, groups, tiles, *refs):
    refs, out, sources = refs[:-2], refs[-2], refs[-1]
    size = tiles.shape[1]
    before = None
    if refs[0].shape == out.shape:
        before, refs = refs[0], refs[1:]
    blocks = refs[0].shape[0]
    room = order.shape[0] // KINDS

    def place_block(b, carry):
        for k, piece in enumerate(refs):
            sources[k * blocks + b] = piece[b]
        return carry

    lax.fori_loop(0, blocks, place_block, 0)
    sources[EMPTY] = jnp.zeros((size, size), jnp.bfloat16)

    out[...] = jnp.zeros_like(out) if before is None else before[...]
    first, both = groups[kind], groups[kind] + groups[kind + 1]

    def product(q):
        r = jnp.where(q < first, 0, 1)
        at = (kind + r) * room + (q - r * first) * GROUP
        left = jnp.concatenate([tiles[order[at + k]] for k in range(GROUP)], axis=1)
        right = jnp.concatenate([sources[spot[at + k]] for k in range(GROUP)], axis=0)
        rows = pl.ds(pl.multiple_of(r * size, size), size)
        return rows, jnp.dot(left, right, preferred_element_type=jnp.float32)

    def step(i, carry):
        for rows, value in [product(2 * i), product(2 * i + 1)]:
            out[rows] += value
        return carry

    lax.fori_loop(0, (both + 1) // 2, step, 0)


def dense_kernel(core, order, mine, theirs, weight, bias, cotangent, act, keep, send):
    nodes = mine.shape[0]
    part = weight.shape[0] // 2
    hidden = (mine[...] + theirs[...]).astype(jnp.bfloat16)
    where = jnp.concatenate([order[0:1], order[1:2]], axis=1) & (nodes - 1)
    put = (lax.broadcasted_iota(jnp.int32, (nodes, nodes), 0) == where).astype(jnp.bfloat16)
    hidden = jnp.dot(put, hidden, preferred_element_type=jnp.float32).astype(jnp.bfloat16)
    pre_act = jnp.dot(hidden, weight[...], preferred_element_type=jnp.float32) + bias[...]
    sigma = 1.0 / (1.0 + jnp.exp(-pre_act))
    act[...] = (pre_act * sigma).astype(jnp.bfloat16)
    slope = sigma * (1.0 + pre_act * (1.0 - sigma))
    scaled = (cotangent[...].astype(jnp.float32) * slope).astype(jnp.bfloat16)
    total = lax.dot_general(
        hidden, scaled, (((0,), (0,)), ((), ())), preferred_element_type=jnp.float32
    )
    column = jnp.sum(scaled.astype(jnp.float32), axis=0, keepdims=True)
    lower = core[0] == 0
    keep[:part] = jnp.where(lower, total[:part], total[part:])
    send[:part] = jnp.where(lower, total[part:], total[:part])
    keep[part:] = jnp.broadcast_to(column, (8, total.shape[1]))
    send[part:] = jnp.broadcast_to(column, (8, total.shape[1]))


def finish_kernel(scale, core, own, other, weight_grad, bias_grad):
    part = own.shape[0] - 8
    lower = core[0] == 0
    weight_grad[:part] = jnp.where(lower, own[:part], other[:part]) * scale
    weight_grad[part:] = jnp.where(lower, other[:part], own[:part]) * scale
    bias_grad[...] = jnp.where(lower, own[part : part + 1], other[part : part + 1]) * scale


def kinds_and_places(tile_row, tile_col, me):
    source = tile_col >> 1
    away = source ^ me
    x, y, z, c = (away >> 5) & 3, (away >> 3) & 3, (away >> 1) & 3, away & 1
    flip = (source & 1) == 1
    last, plane = jnp.where(flip, y, x), jnp.where(flip, x, y)
    early = last == 0
    kind = jnp.where(early, 0, 2 + 2 * c) + (tile_row & 1)
    return kind, jnp.where(early, c, last - 1) * 16 + plane * 4 + z


def aggregated(own, me, tile_vals, tile_row, tile_col, tile_count):
    slots, size, _ = tile_vals.shape
    width = own.shape[1]

    def products(kind, before, pieces):
        before = [] if before is None else [before]
        return pl.pallas_call(
            functools.partial(tiles_kernel, kind),
            out_shape=jax.ShapeDtypeStruct((2 * size, width), jnp.float32),
            in_specs=[SMEM] * 3 + [VMEM] * (1 + len(before) + len(pieces)),
            out_specs=VMEM,
            scratch_shapes=[pltpu.VMEM((EMPTY + 1, size, width), jnp.bfloat16)],
            compiler_params=pltpu.CompilerParams(vmem_limit_bytes=8 * 2**20),
            cost_estimate=pl.CostEstimate(
                flops=128 * size**3, bytes_accessed=64 * 2 * size**2, transcendentals=0
            ),
        )(*plan, tile_vals, *before, *pieces)

    line = jnp.concatenate([own[None]] + [swap(own[None], "z", s) for s in (1, 2, 3)])
    line = lax.optimization_barrier(line)
    plane = jnp.concatenate([line] + [swap_by_core(line, ("y", "x"), s) for s in (1, 2, 3)])
    plane = lax.optimization_barrier(plane)
    one, two, three = (swap_by_core(plane, ("x", "y"), s) for s in (1, 2, 3))
    other = swap(plane, "c", 1)

    row, col, _ = lax.optimization_barrier((tile_row, tile_col, plane))
    kind, place = kinds_and_places(row, col, me)
    entries = jax.ShapeDtypeStruct((KINDS * (slots + 2 * GROUP),), jnp.int32)
    plan = pl.pallas_call(
        plan_kernel,
        out_shape=(entries, entries, jax.ShapeDtypeStruct((KINDS,), jnp.int32)),
        in_specs=[SMEM] * 3,
        out_specs=(SMEM,) * 3,
        scratch_shapes=[pltpu.SMEM((KINDS,), jnp.int32)],
        compiler_params=pltpu.CompilerParams(vmem_limit_bytes=4 * 2**20),
    )(kind, place, tile_count)
    total = products(0, None, [plane, other])
    one, two, three, total = lax.optimization_barrier((one, two, three, total))
    others = [swap(p, "c", 1) for p in (one, two, three)]
    total = products(2, total, [one, two, three])
    return products(4, total, others)


def body(features, node_order, tile_vals, tile_row, tile_col, tile_count, weight, bias, cotangent):
    nodes, width = features.shape
    hid = weight.shape[1]
    part = width // 2
    me = lax.axis_index(ROWS)
    core = lax.axis_index("c").reshape(1)
    rep = lax.axis_index("rep").reshape(1)
    order = node_order.reshape(2, nodes // 2)
    own = pl.pallas_call(
        reorder_kernel,
        out_shape=jax.ShapeDtypeStruct((nodes // 2, width), jnp.bfloat16),
        in_specs=[SMEM, VMEM, VMEM],
        out_specs=VMEM,
        compiler_params=pltpu.CompilerParams(vmem_limit_bytes=56 * 2**20),
    )(rep, order, features)

    mine = aggregated(own, me, tile_vals, tile_row, tile_col, tile_count)
    theirs = swap(mine, "rep", 1)
    act, keep, send = pl.pallas_call(
        dense_kernel,
        out_shape=(
            jax.ShapeDtypeStruct((nodes, hid), jnp.bfloat16),
            jax.ShapeDtypeStruct((part + 8, hid), jnp.float32),
            jax.ShapeDtypeStruct((part + 8, hid), jnp.float32),
        ),
        in_specs=[SMEM] + [VMEM] * 6,
        out_specs=(VMEM,) * 3,
        compiler_params=pltpu.CompilerParams(vmem_limit_bytes=16 * 2**20),
    )(core, order, mine, theirs, weight, bias.reshape(1, hid), cotangent)
    total = keep + swap(send, "c", 1)
    for axes in (("z", "x"), ("y", "z"), ("x", "y")):
        one, two, three = (swap_by_core(total, axes, step) for step in (1, 2, 3))
        total = (total + one) + (two + three)
    scale = float(nodes * lax.axis_size(ROWS)) ** -0.5
    weight_grad, bias_grad = pl.pallas_call(
        functools.partial(finish_kernel, scale),
        out_shape=(
            jax.ShapeDtypeStruct((width, hid), jnp.float32),
            jax.ShapeDtypeStruct((1, hid), jnp.float32),
        ),
        in_specs=[SMEM] + [VMEM] * 2,
        out_specs=(VMEM,) * 2,
        compiler_params=pltpu.CompilerParams(vmem_limit_bytes=4 * 2**20),
    )(core, total, swap(total, "c", 1))
    return act, weight_grad, bias_grad.reshape(hid)


def solution(mesh):
    finer = Mesh(mesh.devices.reshape(4, 4, 4, 2, mesh.shape["rep"]), ROWS_REP)
    return jax.shard_map(
        body,
        mesh=finer,
        in_specs=(
            P(ROWS, None),
            P(ROWS),
            P(ROWS_REP, None, None),
            P(ROWS_REP),
            P(ROWS_REP),
            P(ROWS_REP),
            P(),
            P(),
            P(ROWS, None),
        ),
        out_specs=(P(ROWS, None), P(), P()),
        check_vma=False,
    )
```

```python
import functools
import itertools

import jax
import jax.numpy as jnp
from jax import lax
from jax.experimental import pallas as pl
from jax.experimental.pallas import tpu as pltpu
from jax.sharding import Mesh
from jax.sharding import PartitionSpec as P

ROWS = ("x", "y", "z", "c")
ROWS_REP = ("x", "y", "z", "c", "rep")
GROUP = 8
KINDS = 6
EMPTY = 48

SMEM = pl.BlockSpec(memory_space=pltpu.SMEM)
VMEM = pl.BlockSpec(memory_space=pltpu.VMEM)


def swap(value, axis, step):
    n = lax.axis_size(axis)
    return lax.ppermute(value, axis, [(i, i ^ step) for i in range(n)])


def swap_by_core(value, axes, step):
    names = ("x", "y", "z", "c")
    shape = [lax.axis_size(name) for name in names]
    pairs = []
    for source, index in enumerate(itertools.product(*map(range, shape))):
        at = names.index(axes[index[3]])
        target = 0
        for place, (size, i) in enumerate(zip(shape, index)):
            target = target * size + (i ^ step if place == at else i)
        pairs.append((source, target))
    return lax.ppermute(value, names, pairs)


def reorder_kernel(rep, order, features, own):
    half = own.shape[0]
    nodes = features.shape[0]
    wanted = order[pl.ds(rep[0], 1), :] & (nodes - 1)
    pick = (lax.broadcasted_iota(jnp.int32, (nodes, half), 0) == wanted).astype(jnp.bfloat16)
    own[...] = lax.dot_general(
        pick, features[...], (((0,), (0,)), ((), ())), preferred_element_type=jnp.float32
    ).astype(jnp.bfloat16)


def copy_kernel(source, target):
    target[...] = source[...]


def plan_kernel(kind, place, count, order, spot, groups, filled):
    room = order.shape[0] // KINDS
    for n in range(KINDS):
        filled[n] = n * room

    def step(t, carry):
        n = kind[t]
        at = filled[n]
        order[at] = t
        spot[at] = place[t]
        filled[n] = at + 1
        return carry

    lax.fori_loop(0, count[0], step, 0)

    def finish(n, carry):
        end = filled[n]
        for k in range(2 * GROUP):
            order[end + k] = 0
            spot[end + k] = EMPTY
        groups[n] = (end - n * room + GROUP - 1) // GROUP
        return carry

    lax.fori_loop(0, KINDS, finish, 0)


def tiles_kernel(kind, order, spot, groups, tiles, *refs):
    refs, out, sources = refs[:-2], refs[-2], refs[-1]
    size = tiles.shape[1]
    before = None
    if refs[0].shape == out.shape:
        before, refs = refs[0], refs[1:]
    blocks = refs[0].shape[0]
    room = order.shape[0] // KINDS

    def place_block(b, carry):
        for k, piece in enumerate(refs):
            sources[k * blocks + b] = piece[b]
        return carry

    lax.fori_loop(0, blocks, place_block, 0)
    sources[EMPTY] = jnp.zeros((size, size), jnp.bfloat16)

    out[...] = jnp.zeros_like(out) if before is None else before[...]
    first, both = groups[kind], groups[kind] + groups[kind + 1]

    def product(q):
        r = jnp.where(q < first, 0, 1)
        at = (kind + r) * room + (q - r * first) * GROUP
        left = jnp.concatenate([tiles[order[at + k]] for k in range(GROUP)], axis=1)
        right = jnp.concatenate([sources[spot[at + k]] for k in range(GROUP)], axis=0)
        rows = pl.ds(pl.multiple_of(r * size, size), size)
        return rows, jnp.dot(left, right, preferred_element_type=jnp.float32)

    def step(i, carry):
        for rows, value in [product(2 * i), product(2 * i + 1)]:
            out[rows] += value
        return carry

    lax.fori_loop(0, (both + 1) // 2, step, 0)


def dense_kernel(core, order, mine, theirs, weight, bias, cotangent, act, keep, send):
    nodes = mine.shape[0]
    part = weight.shape[0] // 2
    hidden = (mine[...] + theirs[...]).astype(jnp.bfloat16)
    where = jnp.concatenate([order[0:1], order[1:2]], axis=1) & (nodes - 1)
    put = (lax.broadcasted_iota(jnp.int32, (nodes, nodes), 0) == where).astype(jnp.bfloat16)
    hidden = jnp.dot(put, hidden, preferred_element_type=jnp.float32).astype(jnp.bfloat16)
    pre_act = jnp.dot(hidden, weight[...], preferred_element_type=jnp.float32) + bias[...]
    sigma = 1.0 / (1.0 + jnp.exp(-pre_act))
    act[...] = (pre_act * sigma).astype(jnp.bfloat16)
    slope = sigma * (1.0 + pre_act * (1.0 - sigma))
    scaled = (cotangent[...].astype(jnp.float32) * slope).astype(jnp.bfloat16)
    total = lax.dot_general(
        hidden, scaled, (((0,), (0,)), ((), ())), preferred_element_type=jnp.float32
    )
    column = jnp.sum(scaled.astype(jnp.float32), axis=0, keepdims=True)
    lower = core[0] == 0
    keep[:part] = jnp.where(lower, total[:part], total[part:])
    send[:part] = jnp.where(lower, total[part:], total[:part])
    keep[part:] = jnp.broadcast_to(column, (8, total.shape[1]))
    send[part:] = jnp.broadcast_to(column, (8, total.shape[1]))


def finish_kernel(scale, core, own, other, weight_grad, bias_grad):
    part = own.shape[0] - 8
    lower = core[0] == 0
    weight_grad[:part] = jnp.where(lower, own[:part], other[:part]) * scale
    weight_grad[part:] = jnp.where(lower, other[:part], own[:part]) * scale
    bias_grad[...] = jnp.where(lower, own[part : part + 1], other[part : part + 1]) * scale


def kinds_and_places(tile_row, tile_col, me):
    source = tile_col >> 1
    away = source ^ me
    x, y, z, c = (away >> 5) & 3, (away >> 3) & 3, (away >> 1) & 3, away & 1
    flip = (source & 1) == 1
    last, plane = jnp.where(flip, y, x), jnp.where(flip, x, y)
    early = last == 0
    kind = jnp.where(early, 0, 2 + 2 * c) + (tile_row & 1)
    return kind, jnp.where(early, c, last - 1) * 16 + plane * 4 + z


def aggregated(own, me, tile_vals, tile_row, tile_col, tile_count):
    slots, size, _ = tile_vals.shape
    width = own.shape[1]

    def products(kind, before, pieces):
        before = [] if before is None else [before]
        return pl.pallas_call(
            functools.partial(tiles_kernel, kind),
            out_shape=jax.ShapeDtypeStruct((2 * size, width), jnp.float32),
            in_specs=[SMEM] * 3 + [VMEM] * (1 + len(before) + len(pieces)),
            out_specs=VMEM,
            scratch_shapes=[pltpu.VMEM((EMPTY + 1, size, width), jnp.bfloat16)],
            compiler_params=pltpu.CompilerParams(vmem_limit_bytes=8 * 2**20),
            cost_estimate=pl.CostEstimate(
                flops=128 * size**3, bytes_accessed=64 * 2 * size**2, transcendentals=0
            ),
        )(*plan, tile_vals, *before, *pieces)

    here = pl.pallas_call(
        copy_kernel,
        out_shape=jax.ShapeDtypeStruct((1, *own.shape), own.dtype),
        in_specs=[VMEM],
        out_specs=VMEM,
        compiler_params=pltpu.CompilerParams(vmem_limit_bytes=4 * 2**20),
    )(own[None])
    line = jnp.concatenate([here] + [swap(own[None], "z", s) for s in (1, 2, 3)])
    line = lax.optimization_barrier(line)
    plane = jnp.concatenate([line] + [swap_by_core(line, ("y", "x"), s) for s in (1, 2, 3)])
    plane = lax.optimization_barrier(plane)
    one, two, three = (swap_by_core(plane, ("x", "y"), s) for s in (1, 2, 3))
    other = swap(plane, "c", 1)

    row, col, _ = lax.optimization_barrier((tile_row, tile_col, plane))
    kind, place = kinds_and_places(row, col, me)
    entries = jax.ShapeDtypeStruct((KINDS * (slots + 2 * GROUP),), jnp.int32)
    plan = pl.pallas_call(
        plan_kernel,
        out_shape=(entries, entries, jax.ShapeDtypeStruct((KINDS,), jnp.int32)),
        in_specs=[SMEM] * 3,
        out_specs=(SMEM,) * 3,
        scratch_shapes=[pltpu.SMEM((KINDS,), jnp.int32)],
        compiler_params=pltpu.CompilerParams(vmem_limit_bytes=4 * 2**20),
    )(kind, place, tile_count)
    total = products(0, None, [plane, other])
    three, total = lax.optimization_barrier((three, total))
    others = [swap(p, "c", 1) for p in (one, two, three)]
    total = products(2, total, [one, two, three])
    return products(4, total, others)


def body(features, node_order, tile_vals, tile_row, tile_col, tile_count, weight, bias, cotangent):
    nodes, width = features.shape
    hid = weight.shape[1]
    part = width // 2
    me = lax.axis_index(ROWS)
    core = lax.axis_index("c").reshape(1)
    rep = lax.axis_index("rep").reshape(1)
    order = node_order.reshape(2, nodes // 2)
    own = pl.pallas_call(
        reorder_kernel,
        out_shape=jax.ShapeDtypeStruct((nodes // 2, width), jnp.bfloat16),
        in_specs=[SMEM, VMEM, VMEM],
        out_specs=VMEM,
        compiler_params=pltpu.CompilerParams(vmem_limit_bytes=56 * 2**20),
    )(rep, order, features)

    mine = aggregated(own, me, tile_vals, tile_row, tile_col, tile_count)
    theirs = swap(mine, "rep", 1)
    act, keep, send = pl.pallas_call(
        dense_kernel,
        out_shape=(
            jax.ShapeDtypeStruct((nodes, hid), jnp.bfloat16),
            jax.ShapeDtypeStruct((part + 8, hid), jnp.float32),
            jax.ShapeDtypeStruct((part + 8, hid), jnp.float32),
        ),
        in_specs=[SMEM] + [VMEM] * 6,
        out_specs=(VMEM,) * 3,
        compiler_params=pltpu.CompilerParams(vmem_limit_bytes=16 * 2**20),
    )(core, order, mine, theirs, weight, bias.reshape(1, hid), cotangent)
    total = keep + swap(send, "c", 1)
    for axes in (("z", "x"), ("y", "z"), ("x", "y")):
        one, two, three = (swap_by_core(total, axes, step) for step in (1, 2, 3))
        total = (total + one) + (two + three)
    scale = float(nodes * lax.axis_size(ROWS)) ** -0.5
    weight_grad, bias_grad = pl.pallas_call(
        functools.partial(finish_kernel, scale),
        out_shape=(
            jax.ShapeDtypeStruct((width, hid), jnp.float32),
            jax.ShapeDtypeStruct((1, hid), jnp.float32),
        ),
        in_specs=[SMEM] + [VMEM] * 2,
        out_specs=(VMEM,) * 2,
        compiler_params=pltpu.CompilerParams(vmem_limit_bytes=4 * 2**20),
    )(core, total, swap(total, "c", 1))
    return act, weight_grad, bias_grad.reshape(hid)


def solution(mesh):
    finer = Mesh(mesh.devices.reshape(4, 4, 4, 2, mesh.shape["rep"]), ROWS_REP)
    return jax.shard_map(
        body,
        mesh=finer,
        in_specs=(
            P(ROWS, None),
            P(ROWS),
            P(ROWS_REP, None, None),
            P(ROWS_REP),
            P(ROWS_REP),
            P(ROWS_REP),
            P(),
            P(),
            P(ROWS, None),
        ),
        out_specs=(P(ROWS, None), P(), P()),
        check_vma=False,
    )
```

```python
import functools
import itertools

import jax
import jax.numpy as jnp
from jax import lax
from jax.experimental import pallas as pl
from jax.experimental.pallas import tpu as pltpu
from jax.sharding import Mesh
from jax.sharding import PartitionSpec as P

ROWS = ("x", "y", "z", "c")
ROWS_REP = ("x", "y", "z", "c", "rep")
GROUP = 8
KINDS = 6
EMPTY = 48

SMEM = pl.BlockSpec(memory_space=pltpu.SMEM)
VMEM = pl.BlockSpec(memory_space=pltpu.VMEM)


def swap(value, axis, step):
    n = lax.axis_size(axis)
    return lax.ppermute(value, axis, [(i, i ^ step) for i in range(n)])


def swap_by_core(value, axes, step):
    names = ("x", "y", "z", "c")
    shape = [lax.axis_size(name) for name in names]
    pairs = []
    for source, index in enumerate(itertools.product(*map(range, shape))):
        at = names.index(axes[index[3]])
        target = 0
        for place, (size, i) in enumerate(zip(shape, index)):
            target = target * size + (i ^ step if place == at else i)
        pairs.append((source, target))
    return lax.ppermute(value, names, pairs)


def reorder_kernel(order, features, own):
    half = own.shape[0]
    nodes = features.shape[0]
    wanted = order[pl.ds(lax.axis_index("rep"), 1), :] & (nodes - 1)
    pick = (lax.broadcasted_iota(jnp.int32, (nodes, half), 0) == wanted).astype(jnp.bfloat16)
    own[...] = lax.dot_general(
        pick, features[...], (((0,), (0,)), ((), ())), preferred_element_type=jnp.float32
    ).astype(jnp.bfloat16)


def copy_kernel(source, target):
    target[...] = source[...]


def plan_kernel(kind, place, count, order, spot, groups, filled):
    room = order.shape[0] // KINDS
    for n in range(KINDS):
        filled[n] = n * room

    def step(t, carry):
        n = kind[t]
        at = filled[n]
        order[at] = t
        spot[at] = place[t]
        filled[n] = at + 1
        return carry

    lax.fori_loop(0, count[0], step, 0)

    def finish(n, carry):
        end = filled[n]
        for k in range(2 * GROUP):
            order[end + k] = 0
            spot[end + k] = EMPTY
        groups[n] = (end - n * room + GROUP - 1) // GROUP
        return carry

    lax.fori_loop(0, KINDS, finish, 0)


def tiles_kernel(kind, order, spot, groups, tiles, *refs):
    refs, out, sources = refs[:-2], refs[-2], refs[-1]
    size = tiles.shape[1]
    before = None
    if refs[0].shape == out.shape:
        before, refs = refs[0], refs[1:]
    blocks = refs[0].shape[0]
    room = order.shape[0] // KINDS

    def place_block(b, carry):
        for k, piece in enumerate(refs):
            sources[k * blocks + b] = piece[b]
        return carry

    lax.fori_loop(0, blocks, place_block, 0)
    sources[EMPTY] = jnp.zeros((size, size), jnp.bfloat16)

    out[...] = jnp.zeros_like(out) if before is None else before[...]
    first, both = groups[kind], groups[kind] + groups[kind + 1]

    def product(q):
        r = jnp.where(q < first, 0, 1)
        at = (kind + r) * room + (q - r * first) * GROUP
        left = jnp.concatenate([tiles[order[at + k]] for k in range(GROUP)], axis=1)
        right = jnp.concatenate([sources[spot[at + k]] for k in range(GROUP)], axis=0)
        rows = pl.ds(pl.multiple_of(r * size, size), size)
        return rows, jnp.dot(left, right, preferred_element_type=jnp.float32)

    def step(i, carry):
        for rows, value in [product(2 * i), product(2 * i + 1)]:
            out[rows] += value
        return carry

    lax.fori_loop(0, (both + 1) // 2, step, 0)


def dense_kernel(core, order, mine, theirs, weight, bias, cotangent, act, keep, send):
    nodes = mine.shape[0]
    part = weight.shape[0] // 2
    hidden = (mine[...] + theirs[...]).astype(jnp.bfloat16)
    where = jnp.concatenate([order[0:1], order[1:2]], axis=1) & (nodes - 1)
    put = (lax.broadcasted_iota(jnp.int32, (nodes, nodes), 0) == where).astype(jnp.bfloat16)
    hidden = jnp.dot(put, hidden, preferred_element_type=jnp.float32).astype(jnp.bfloat16)
    pre_act = jnp.dot(hidden, weight[...], preferred_element_type=jnp.float32) + bias[...]
    sigma = 1.0 / (1.0 + jnp.exp(-pre_act))
    act[...] = (pre_act * sigma).astype(jnp.bfloat16)
    slope = sigma * (1.0 + pre_act * (1.0 - sigma))
    scaled = (cotangent[...].astype(jnp.float32) * slope).astype(jnp.bfloat16)
    total = lax.dot_general(
        hidden, scaled, (((0,), (0,)), ((), ())), preferred_element_type=jnp.float32
    )
    column = jnp.sum(scaled.astype(jnp.float32), axis=0, keepdims=True)
    lower = core[0] == 0
    keep[:part] = jnp.where(lower, total[:part], total[part:])
    send[:part] = jnp.where(lower, total[part:], total[:part])
    keep[part:] = jnp.broadcast_to(column, (8, total.shape[1]))
    send[part:] = jnp.broadcast_to(column, (8, total.shape[1]))


def finish_kernel(scale, core, own, other, weight_grad, bias_grad):
    part = own.shape[0] - 8
    lower = core[0] == 0
    weight_grad[:part] = jnp.where(lower, own[:part], other[:part]) * scale
    weight_grad[part:] = jnp.where(lower, other[:part], own[:part]) * scale
    bias_grad[...] = jnp.where(lower, own[part : part + 1], other[part : part + 1]) * scale


def kinds_and_places(tile_row, tile_col, me):
    source = tile_col >> 1
    away = source ^ me
    x, y, z, c = (away >> 5) & 3, (away >> 3) & 3, (away >> 1) & 3, away & 1
    flip = (source & 1) == 1
    last, plane = jnp.where(flip, y, x), jnp.where(flip, x, y)
    early = last == 0
    kind = jnp.where(early, 0, 2 + 2 * c) + (tile_row & 1)
    return kind, jnp.where(early, c, last - 1) * 16 + plane * 4 + z


def aggregated(own, me, tile_vals, tile_row, tile_col, tile_count):
    slots, size, _ = tile_vals.shape
    width = own.shape[1]

    def products(kind, before, pieces):
        before = [] if before is None else [before]
        return pl.pallas_call(
            functools.partial(tiles_kernel, kind),
            out_shape=jax.ShapeDtypeStruct((2 * size, width), jnp.float32),
            in_specs=[SMEM] * 3 + [VMEM] * (1 + len(before) + len(pieces)),
            out_specs=VMEM,
            scratch_shapes=[pltpu.VMEM((EMPTY + 1, size, width), jnp.bfloat16)],
            compiler_params=pltpu.CompilerParams(vmem_limit_bytes=8 * 2**20),
            cost_estimate=pl.CostEstimate(
                flops=128 * size**3, bytes_accessed=64 * 2 * size**2, transcendentals=0
            ),
        )(*plan, tile_vals, *before, *pieces)

    here = pl.pallas_call(
        copy_kernel,
        out_shape=jax.ShapeDtypeStruct((1, *own.shape), own.dtype),
        in_specs=[VMEM],
        out_specs=VMEM,
        compiler_params=pltpu.CompilerParams(vmem_limit_bytes=4 * 2**20),
    )(own[None])
    line = jnp.concatenate([here] + [swap(own[None], "z", s) for s in (1, 2, 3)])
    line = lax.optimization_barrier(line)
    plane = jnp.concatenate([line] + [swap_by_core(line, ("y", "x"), s) for s in (1, 2, 3)])
    plane = lax.optimization_barrier(plane)
    one, two, three = (swap_by_core(plane, ("x", "y"), s) for s in (1, 2, 3))
    other = swap(plane, "c", 1)

    row, col, _ = lax.optimization_barrier((tile_row, tile_col, plane))
    kind, place = kinds_and_places(row, col, me)
    entries = jax.ShapeDtypeStruct((KINDS * (slots + 2 * GROUP),), jnp.int32)
    plan = pl.pallas_call(
        plan_kernel,
        out_shape=(entries, entries, jax.ShapeDtypeStruct((KINDS,), jnp.int32)),
        in_specs=[SMEM] * 3,
        out_specs=(SMEM,) * 3,
        scratch_shapes=[pltpu.SMEM((KINDS,), jnp.int32)],
        compiler_params=pltpu.CompilerParams(vmem_limit_bytes=4 * 2**20),
    )(kind, place, tile_count)
    total = products(0, None, [plane, other])
    three, total = lax.optimization_barrier((three, total))
    others = [swap(p, "c", 1) for p in (one, two, three)]
    total = products(2, total, [one, two, three])
    return products(4, total, others)


def body(features, node_order, tile_vals, tile_row, tile_col, tile_count, weight, bias, cotangent):
    nodes, width = features.shape
    hid = weight.shape[1]
    part = width // 2
    me = lax.axis_index(ROWS)
    core = lax.axis_index("c").reshape(1)
    order = node_order.reshape(2, nodes // 2)
    own = pl.pallas_call(
        reorder_kernel,
        out_shape=jax.ShapeDtypeStruct((nodes // 2, width), jnp.bfloat16),
        in_specs=[VMEM, VMEM],
        out_specs=VMEM,
        compiler_params=pltpu.CompilerParams(vmem_limit_bytes=56 * 2**20),
    )(order, features)

    mine = aggregated(own, me, tile_vals, tile_row, tile_col, tile_count)
    theirs = swap(mine, "rep", 1)
    act, keep, send = pl.pallas_call(
        dense_kernel,
        out_shape=(
            jax.ShapeDtypeStruct((nodes, hid), jnp.bfloat16),
            jax.ShapeDtypeStruct((part + 8, hid), jnp.float32),
            jax.ShapeDtypeStruct((part + 8, hid), jnp.float32),
        ),
        in_specs=[SMEM] + [VMEM] * 6,
        out_specs=(VMEM,) * 3,
        compiler_params=pltpu.CompilerParams(vmem_limit_bytes=16 * 2**20),
    )(core, order, mine, theirs, weight, bias.reshape(1, hid), cotangent)
    total = keep + swap(send, "c", 1)
    for axes in (("z", "x"), ("y", "z"), ("x", "y")):
        one, two, three = (swap_by_core(total, axes, step) for step in (1, 2, 3))
        total = (total + one) + (two + three)
    scale = float(nodes * lax.axis_size(ROWS)) ** -0.5
    weight_grad, bias_grad = pl.pallas_call(
        functools.partial(finish_kernel, scale),
        out_shape=(
            jax.ShapeDtypeStruct((width, hid), jnp.float32),
            jax.ShapeDtypeStruct((1, hid), jnp.float32),
        ),
        in_specs=[SMEM] + [VMEM] * 2,
        out_specs=(VMEM,) * 2,
        compiler_params=pltpu.CompilerParams(vmem_limit_bytes=4 * 2**20),
    )(core, total, swap(total, "c", 1))
    return act, weight_grad, bias_grad.reshape(hid)


def solution(mesh):
    finer = Mesh(mesh.devices.reshape(4, 4, 4, 2, mesh.shape["rep"]), ROWS_REP)
    return jax.shard_map(
        body,
        mesh=finer,
        in_specs=(
            P(ROWS, None),
            P(ROWS),
            P(ROWS_REP, None, None),
            P(ROWS_REP),
            P(ROWS_REP),
            P(ROWS_REP),
            P(),
            P(),
            P(ROWS, None),
        ),
        out_specs=(P(ROWS, None), P(), P()),
        check_vma=False,
    )
```
